256 devices in a mesh: img: 32 (over y, z_lo, core), txt: 8 (over x, z_hi).
Axes of the slice: x: 4, y: 4, z: 8 (z_hi: 2, z_lo: 4; z = z_hi * 4 + z_lo), core: 2. Of those that a mesh axis runs over, the one named last changes fastest.
Arguments:
- images: bfloat16 [16384, 1152], P(('img', 'txt')), may hold values from -6 to 6
- texts: bfloat16 [16384, 1152], P(('img', 'txt')), may hold values from -6 to 6
- log_scale: float32 [], replicated, may hold values from 2 to 3
- bias: float32 [], replicated, may hold values from -3 to -1
Outputs:
- mean_loss: float32 [], replicated
- grad_images: float32 [16384, 1152], P(('img', 'txt'))
- grad_texts: float32 [16384, 1152], P(('img', 'txt'))
- grad_log_scale: float32 [], replicated
- grad_bias: float32 [], replicated
The draws below stay inside these ranges and needn't reach their ends.
All inputs are finite; a program needn't handle non-finite values.
Results may differ from the reference program's by a relative error of at most 0.0009.
The reference program's roundings to bfloat16 on the way (of `img_low` and `weights`) count: a program that leaves them out, or rounds other values in their place, can miss the bound.
Values may be sent and summed in bfloat16 or wider, within the bound.
No kernel may reach another device: no remote copies, remote signals or barrier semaphores. Data moves between devices by JAX's collectives and lax.ppermute only.
A program may use at most 64 MiB of HBM per device.

```python
import jax
import jax.numpy as jnp
from jax import lax

D = 1152
BATCH = 16384
IMG_ROWS = 512
N_IMG = 32


def block_scale(own_key, dims, shards, low, top_value):
    gain = 1.0
    for dim, blocks in shards:
        heights = jax.random.uniform(jax.random.fold_in(jax.random.fold_in(own_key, 6), dim), (blocks,), jnp.float32, low / len(shards), top_value / len(shards))
        gain = gain * jnp.repeat(jnp.exp(heights), dims[dim] // blocks).reshape((-1,) + (1,) * (len(dims) - 1 - dim))
    return gain


def noise(rng, dims, width, limit, cuts=(), kind=jnp.bfloat16):
    array = width * jax.random.normal(rng, dims, jnp.float32)
    if cuts:
        array = array * block_scale(rng, dims, cuts, -0.22, 0.18)
    return jnp.clip(array, -limit, limit).astype(kind)


def setup_inputs(seed: int = 0) -> dict:
    key_list = jax.random.split(jax.random.key(seed), 5)
    return {
        "images": noise(key_list[0], (BATCH, D), 1.0, 6.0, ((0, 256),)),
        "texts": noise(key_list[1], (BATCH, D), 1.0, 6.0, ((0, 256),)),
        "log_scale": jnp.clip(jax.random.uniform(key_list[2], (), jnp.float32, 2.0, 3.0), 2.0, 3.0),
        "bias": jnp.clip(jax.random.uniform(key_list[3], (), jnp.float32, -3.0, -1.0), -3.0, -1.0),
    }


tiny_eps = 1e-06

def unit_rows(values):
    wide = values.astype(jnp.float32)
    lengths = jnp.sqrt(lax.optimization_barrier(jnp.sum(wide * wide, axis=-1, keepdims=True)) + tiny_eps)
    return (wide / lengths, lengths)

def project_back(unit, direction, lengths):
    along = lax.optimization_barrier(jnp.sum(unit * direction, axis=-1, keepdims=True))
    return (direction - unit * along) / lengths

def reference(images, texts, log_scale, bias):
    unit_img, img_len = unit_rows(images)
    unit_txt, txt_len = unit_rows(texts)
    img_low = unit_img.astype(jnp.bfloat16)
    txt_low = unit_txt.astype(jnp.bfloat16)
    scale = jnp.exp(log_scale)
    columns = jnp.arange(BATCH, dtype=jnp.int32)
    blocks = img_low.reshape(N_IMG, IMG_ROWS, D)

    def step(carry, inputs):
        text_acc, loss_acc, slope_acc, curve_acc = carry
        index, block = inputs
        dots = lax.dot_general(block, txt_low, (((1,), (1,)), ((), ())), preferred_element_type=jnp.float32)
        logits = scale * dots + bias
        rows = index * IMG_ROWS + jnp.arange(IMG_ROWS, dtype=jnp.int32)
        sign = jnp.where(rows[:, None] == columns[None, :], jnp.float32(1.0), jnp.float32(-1.0))
        losses = -jax.nn.log_sigmoid(sign * logits)
        slopes = -sign * jax.nn.sigmoid(-sign * logits)
        weights = (scale * slopes).astype(jnp.bfloat16)
        img_part = jnp.dot(weights, txt_low, preferred_element_type=jnp.float32)
        text_acc = text_acc + lax.dot_general(weights, block, (((0,), (0,)), ((), ())), preferred_element_type=jnp.float32)
        carry = (text_acc, loss_acc + jnp.sum(losses), slope_acc + jnp.sum(slopes), curve_acc + jnp.sum(slopes * dots))
        return (carry, img_part)
    zero = jnp.zeros((), jnp.float32)
    start = (jnp.zeros((BATCH, D), jnp.float32), zero, zero, zero)
    final, img_parts = lax.scan(step, start, (jnp.arange(N_IMG, dtype=jnp.int32), blocks))
    text_dir, loss_sum, slope_sum, curve_sum = final
    img_dir = img_parts.reshape(BATCH, D)
    count = float(BATCH) * float(BATCH)
    grad_images = project_back(unit_img, img_dir, img_len)
    grad_texts = project_back(unit_txt, text_dir, txt_len)
    mean_loss = loss_sum / count
    grad_log_scale = scale * curve_sum / count
    grad_bias = slope_sum / count
    return (mean_loss, grad_images, grad_texts, grad_log_scale, grad_bias)
```

```python
import itertools

import jax
import jax.numpy as jnp
from jax import lax
from jax.experimental import pallas as pl
from jax.experimental.pallas import tpu as pltpu
from jax.sharding import Mesh, PartitionSpec as P

tiny_eps = 1e-06
LOG2E = 1.4426950408889634
LN2 = 0.6931471805599453
F32, BF16, F16 = jnp.float32, jnp.bfloat16, jnp.float16
DOWN, UP = 0.125, 8.0

AXES = ("y", "zl", "c", "x", "zh")
SIZES = (4, 4, 2, 4, 2)
COORDS = list(itertools.product(*[range(s) for s in SIZES]))
PLACE = {coord: n for n, coord in enumerate(COORDS)}


def place(y, z, c, x):
    return PLACE[(y % 4, z % 4, c, x % 4, (z % 8) // 4)]


def permute(move, value):
    pairs = []
    for y, zl, c, x, zh in COORDS:
        z = zh * 4 + zl
        pairs.append((place(y, z, c, x), place(*move(y, z, c, x))))
    return lax.ppermute(value, AXES, pairs)


def first(k, v):
    return permute(lambda y, z, c, x: (y, z, c, x + k) if c == 0 else (y + k, z, c, x), v)


def second(k, v):
    return permute(lambda y, z, c, x: (y + k, z, c, x) if c == 0 else (y, z, c, x + k), v)


def along_z(k, v):
    return permute(lambda y, z, c, x: (y, z + k, c, x) if c == 0 else (y, z - k, c, x), v)


def sibling(v):
    return permute(lambda y, z, c, x: (y, z, 1 - c, x), v)


def low(sums):
    return (sums * DOWN).astype(F16)


def normalise_kernel(images, texts, img_low, txt_low):
    for src, dst in ((images, img_low), (texts, txt_low)):
        wide = src[...].astype(F32)
        length = jnp.sqrt(jnp.sum(wide * wide, axis=-1, keepdims=True) + tiny_eps)
        dst[...] = (wide / length).astype(BF16)


def fold_rows(value):
    rows, cols = value.shape
    return jnp.sum(value.reshape(rows // 8, 8, cols), axis=0)


def product_rows(value):
    while value.shape[0] > 8:
        half = value.shape[0] // 2
        value = value[:half] * value[half:]
    return value


def pair_kernel(sc, *refs):
    imgs, txts = refs[:9], refs[9:13]
    w_ref, keep, send, sums, x_ref, y_ref = refs[13:]
    at = 0
    for r in imgs:
        x_ref[at : at + r.shape[0], :] = r[...]
        at += r.shape[0]
    at = 0
    for r in txts:
        y_ref[at : at + r.shape[0], :] = r[...]
        at += r.shape[0]
    scale = sc[0]
    bias = sc[1]
    lift = jnp.zeros((8, 256), F32)
    logs = jnp.zeros((8, 256), F32)
    slope_acc = jnp.zeros((8, 256), F32)
    curve_acc = jnp.zeros((8, 256), F32)
    for i in range(4):
        for j in range(4):
            dots = lax.dot_general(
                x_ref[i * 256 : i * 256 + 256, :],
                y_ref[j * 256 : j * 256 + 256, :],
                (((1,), (1,)), ((), ())),
                preferred_element_type=F32,
            )
            z = (scale * dots + bias) * LOG2E
            if i == 0 and j == 0:
                row = lax.broadcasted_iota(jnp.int32, (256, 256), 0)
                col = lax.broadcasted_iota(jnp.int32, (256, 256), 1)
                positive = jnp.logical_and(row == col, row < 64)
                z = jnp.where(positive, -z, z)
            e = jnp.exp2(-jnp.abs(z))
            whole = 1.0 + e
            r = 1.0 / whole
            slope = jnp.where(z >= 0.0, r, e * r)
            if i == 0 and j == 0:
                slope = jnp.where(positive, -slope, slope)
            lift += fold_rows(jnp.maximum(z, 0.0))
            logs += jnp.log(product_rows(whole))
            slope_acc += fold_rows(slope)
            curve_acc += fold_rows(slope * dots)
            w_ref[i * 256 : i * 256 + 256, j * 256 : j * 256 + 256] = (scale * slope).astype(BF16)
    loss = LN2 * jnp.sum(lift) + jnp.sum(logs)
    row = lax.broadcasted_iota(jnp.int32, (8, 128), 0)
    sums[...] = jnp.where(
        row == 0, loss, jnp.where(row == 1, jnp.sum(slope_acc), jnp.where(row == 2, jnp.sum(curve_acc), 0.0))
    )
    for lo, hi in ((576, 800), (800, 1024)):
        part = jnp.dot(w_ref[lo:hi, :], y_ref[...], preferred_element_type=F32)
        send[lo - 576 : hi - 576, :] = part
    for lo, hi in ((0, 192), (192, 384), (384, 576)):
        keep[lo:hi, :] = jnp.dot(w_ref[lo:hi, :], y_ref[...], preferred_element_type=F32)


def text_kernel(w_ref, *refs):
    imgs = refs[:9]
    own, back, fore, over, x_ref = refs[9:]
    at = 0
    for r in imgs:
        x_ref[at : at + r.shape[0], :] = r[...]
        at += r.shape[0]
    for j, out in ((1, back), (2, fore), (3, over), (0, own)):
        part = lax.dot_general(
            w_ref[:, j * 256 : j * 256 + 256],
            x_ref[...],
            (((0,), (0,)), ((), ())),
            preferred_element_type=F32,
        )
        out[...] = part


def project_kernel(images, texts, img_dir, txt_dir, grad_images, grad_texts):
    for src, sums, dst in ((images, img_dir, grad_images), (texts, txt_dir, grad_texts)):
        direction = sums[...]
        wide = src[...].astype(F32)
        length = jnp.sqrt(jnp.sum(wide * wide, axis=-1, keepdims=True) + tiny_eps)
        unit = wide / length
        along = jnp.sum(unit * direction, axis=-1, keepdims=True)
        dst[...] = (direction - unit * along) / length


def shards(images, texts, log_scale, bias):
    rows, d = images.shape
    arr = jax.ShapeDtypeStruct
    img_low, txt_low = pl.pallas_call(
        normalise_kernel, out_shape=(arr((rows, d), BF16), arr((rows, d), BF16)), name="normalise"
    )(images, texts)
    scale = jnp.exp(log_scale)
    scalars = jnp.stack([scale, bias])

    pair = jnp.concatenate([img_low, sibling(img_low)], axis=0)
    r1 = along_z(1, pair)
    r2 = along_z(2, pair)
    a, b, c = first(1, txt_low), first(-1, txt_low), first(2, txt_low)
    block = jnp.concatenate([txt_low, a, b, c], axis=0)
    r3 = along_z(1, r2)
    r4 = along_z(2, r2[:64])
    ta, tb, tc = second(1, block), second(-1, block), second(2, block)
    imgs = (pair, r1, r2, r3, r4, sibling(r1), sibling(r2), sibling(r3), sibling(r4))
    txts = (block, ta, tb, tc)

    vmem = pl.BlockSpec(memory_space=pltpu.VMEM)
    w, keep, send, sums = pl.pallas_call(
        pair_kernel,
        in_specs=[pl.BlockSpec(memory_space=pltpu.SMEM)] + [vmem] * 13,
        out_specs=[vmem] * 4,
        out_shape=(arr((1024, 1024), BF16), arr((576, d), F32), arr((448, d), F32), arr((8, 128), F32)),
        scratch_shapes=[pltpu.VMEM((1024, d), BF16), pltpu.VMEM((1024, d), BF16)],
        compiler_params=pltpu.CompilerParams(vmem_limit_bytes=48 * 1024 * 1024),
        cost_estimate=pl.CostEstimate(flops=4 * 1024 * 1024 * 1152, bytes_accessed=12_000_000, transcendentals=2 * 1024 * 1024),
        name="pairs",
    )(scalars, *imgs, *txts)
    got = sibling(low(send))

    t_own, t_back, t_fore, t_over = pl.pallas_call(
        text_kernel,
        in_specs=[vmem] * 10,
        out_specs=[vmem] * 4,
        out_shape=(arr((256, d), F32),) * 4,
        scratch_shapes=[pltpu.VMEM((1024, d), BF16)],
        compiler_params=pltpu.CompilerParams(vmem_limit_bytes=48 * 1024 * 1024),
        cost_estimate=pl.CostEstimate(flops=2 * 1024 * 1024 * 1152, bytes_accessed=8_000_000, transcendentals=0),
        name="texts",
    )(w, *imgs)

    chain = keep[128:] * DOWN + got.astype(F32)
    g3 = along_z(-1, chain[256:384].astype(F16))
    g4 = along_z(-2, chain[384:448].astype(F16))
    c2 = chain[128:256] + g3.astype(F32) + jnp.pad(g4.astype(F32), ((0, 64), (0, 0)))
    g1 = along_z(-1, chain[0:128].astype(F16))
    g2 = along_z(-2, c2.astype(F16))
    mine = keep[:128] + (g1.astype(F32) + g2.astype(F32)) * UP
    img_dir = mine[:64] + sibling(mine[64:])

    s1, s2, s3 = second(-1, low(t_back)), second(1, low(t_fore)), second(2, low(t_over))
    t_sum = t_own + (s1.astype(F32) + s2.astype(F32) + s3.astype(F32)) * UP
    t_low = low(t_sum[64:])
    f1, f2, f3 = first(-1, t_low[0:64]), first(1, t_low[64:128]), first(2, t_low[128:192])
    txt_dir = t_sum[:64] + (f1.astype(F32) + f2.astype(F32) + f3.astype(F32)) * UP

    grad_images, grad_texts = pl.pallas_call(
        project_kernel, out_shape=(arr((rows, d), F32), arr((rows, d), F32)), name="project"
    )(images, texts, img_dir, txt_dir)

    sums = sums + sibling(sums)
    for bit in (1, 2, 4):
        sums = sums + permute(lambda y, z, c, x: (y, z ^ bit, c, x), sums)
    for bit in (1, 2):
        sums = sums + permute(lambda y, z, c, x: (y ^ bit, z, c, x), sums)
        sums = sums + permute(lambda y, z, c, x: (y, z, c, x ^ bit), sums)
    total = float(rows * 256)
    count = total * total
    return (sums[0, 0] / count, grad_images, grad_texts, scale * sums[2, 0] / count, sums[1, 0] / count)


def solution(mesh):
    fine = Mesh(mesh.devices.reshape(SIZES), AXES)
    rows = P(AXES, None)
    return jax.shard_map(
        shards,
        mesh=fine,
        in_specs=(rows, rows, P(), P()),
        out_specs=(P(), rows, rows, P(), P()),
        check_vma=False,
    )
```

```python
import itertools

import jax
import jax.numpy as jnp
from jax import lax
from jax.experimental import pallas as pl
from jax.experimental.pallas import tpu as pltpu
from jax.sharding import Mesh, PartitionSpec as P

tiny_eps = 1e-06
LOG2E = 1.4426950408889634
LN2 = 0.6931471805599453
F32, BF16, F16 = jnp.float32, jnp.bfloat16, jnp.float16
SHRINK = 2.0**-20
DOWN, UP = 0.125, 8.0

AXES = ("y", "zl", "c", "x", "zh")
SIZES = (4, 4, 2, 4, 2)
COORDS = list(itertools.product(*[range(s) for s in SIZES]))
PLACE = {coord: n for n, coord in enumerate(COORDS)}


def place(y, z, c, x):
    return PLACE[(y % 4, z % 4, c, x % 4, (z % 8) // 4)]


def permute(move, value):
    pairs = []
    for y, zl, c, x, zh in COORDS:
        z = zh * 4 + zl
        pairs.append((place(y, z, c, x), place(*move(y, z, c, x))))
    return lax.ppermute(value, AXES, pairs)


def first(k, v):
    return permute(lambda y, z, c, x: (y, z, c, x + k) if c == 0 else (y + k, z, c, x), v)


def second(k, v):
    return permute(lambda y, z, c, x: (y + k, z, c, x) if c == 0 else (y, z, c, x + k), v)


def along_z(k, v):
    return permute(lambda y, z, c, x: (y, z + k, c, x) if c == 0 else (y, z - k, c, x), v)


def sibling(v):
    return permute(lambda y, z, c, x: (y, z, 1 - c, x), v)


def flip_z(bit, v):
    return permute(lambda y, z, c, x: (y, z ^ bit, c, x), v)


def flip_second(bit, v):
    return permute(lambda y, z, c, x: (y ^ bit, z, c, x) if c == 0 else (y, z, c, x ^ bit), v)


def split(sums):
    value = sums * SHRINK
    terms = []
    for _ in range(3):
        term = lax.reduce_precision(value, 5, 10)
        terms.append(term.astype(F16))
        value = (value - term) * 2048.0
    return jnp.pad(jnp.concatenate(terms, axis=1), ((0, 0), (0, 768)))


def join(codes):
    return (codes[:, :128] + codes[:, 128:256] / 2048.0 + codes[:, 256:384] / 2048.0**2) / SHRINK


def low(sums):
    return (sums * DOWN).astype(F16)


def normalise_kernel(images, texts, img_low, txt_low):
    for src, dst in ((images, img_low), (texts, txt_low)):
        wide = src[...].astype(F32)
        length = jnp.sqrt(jnp.sum(wide * wide, axis=-1, keepdims=True) + tiny_eps)
        dst[...] = (wide / length).astype(BF16)


def fold_rows(value):
    rows, cols = value.shape
    return jnp.sum(value.reshape(rows // 8, 8, cols), axis=0)


def product_rows(value):
    while value.shape[0] > 8:
        half = value.shape[0] // 2
        value = value[:half] * value[half:]
    return value


def lay(pieces, dst):
    at = 0
    for piece in pieces:
        dst[at : at + piece.shape[0], :] = piece[...]
        at += piece.shape[0]


def pair_kernel(sc, *refs):
    imgs, txts = refs[:9], refs[9:13]
    w_ref, x_ref, y_ref, sums = refs[13:]
    lay(imgs, x_ref)
    lay(txts, y_ref)
    scale = sc[0]
    bias = sc[1]
    lift = jnp.zeros((8, 256), F32)
    logs = jnp.zeros((8, 256), F32)
    slope_acc = jnp.zeros((8, 256), F32)
    curve_acc = jnp.zeros((8, 256), F32)
    for j in range(4):
        for i in range(4):
            dots = lax.dot_general(
                x_ref[i * 256 : i * 256 + 256, :],
                y_ref[j * 256 : j * 256 + 256, :],
                (((1,), (1,)), ((), ())),
                preferred_element_type=F32,
            )
            z = (scale * dots + bias) * LOG2E
            if i == 0 and j == 0:
                row = lax.broadcasted_iota(jnp.int32, (256, 256), 0)
                col = lax.broadcasted_iota(jnp.int32, (256, 256), 1)
                positive = jnp.logical_and(row == col, row < 64)
                z = jnp.where(positive, -z, z)
            e = jnp.exp2(-jnp.abs(z))
            whole = 1.0 + e
            r = 1.0 / whole
            slope = jnp.where(z >= 0.0, r, e * r)
            if i == 0 and j == 0:
                slope = jnp.where(positive, -slope, slope)
            lift += fold_rows(jnp.maximum(z, 0.0))
            logs += jnp.log(product_rows(whole))
            slope_acc += fold_rows(slope)
            curve_acc += fold_rows(slope * dots)
            w_ref[i * 256 : i * 256 + 256, j * 256 : j * 256 + 256] = (scale * slope).astype(BF16)
    loss = LN2 * jnp.sum(lift) + jnp.sum(logs)
    row = lax.broadcasted_iota(jnp.int32, (8, 128), 0)
    sums[...] = jnp.where(
        row == 0, loss, jnp.where(row == 1, jnp.sum(slope_acc), jnp.where(row == 2, jnp.sum(curve_acc), 0.0))
    )


def image_kernel(w_ref, y_ref, keep, send):
    for lo, hi in ((576, 800), (800, 1024)):
        send[lo - 576 : hi - 576, :] = jnp.dot(w_ref[lo:hi, :], y_ref[...], preferred_element_type=F32)
    for lo, hi in ((0, 288), (288, 576)):
        keep[lo:hi, :] = jnp.dot(w_ref[lo:hi, :], y_ref[...], preferred_element_type=F32)


def text_kernel(w_ref, x_ref, own, back, fore, over):
    for j, out in ((1, back), (2, fore), (3, over), (0, own)):
        out[...] = lax.dot_general(
            w_ref[:, j * 256 : j * 256 + 256], x_ref[...], (((0,), (0,)), ((), ())), preferred_element_type=F32
        )


def project_kernel(images, texts, img_dir, txt_dir, grad_images, grad_texts):
    for src, sums, dst in ((images, img_dir, grad_images), (texts, txt_dir, grad_texts)):
        direction = sums[...]
        wide = src[...].astype(F32)
        length = jnp.sqrt(jnp.sum(wide * wide, axis=-1, keepdims=True) + tiny_eps)
        unit = wide / length
        along = jnp.sum(unit * direction, axis=-1, keepdims=True)
        dst[...] = (direction - unit * along) / length


def shards(images, texts, log_scale, bias):
    rows, d = images.shape
    arr = jax.ShapeDtypeStruct
    img_low, txt_low = pl.pallas_call(
        normalise_kernel, out_shape=(arr((rows, d), BF16), arr((rows, d), BF16)), name="normalise"
    )(images, texts)
    scale = jnp.exp(log_scale)
    scalars = jnp.stack([scale, bias])

    pair = jnp.concatenate([img_low, sibling(img_low)], axis=0)
    r1 = along_z(1, pair)
    r2 = along_z(2, pair)
    a, b, c = first(1, txt_low), first(-1, txt_low), first(2, txt_low)
    block = jnp.concatenate([txt_low, a, b, c], axis=0)
    block, pair = lax.optimization_barrier((block, pair))
    ta, tb, tc = second(1, block), second(-1, block), second(2, block)
    q1, q2 = sibling(r1), sibling(r2)
    r2, q1, q2 = lax.optimization_barrier((r2, q1, q2))
    r3 = along_z(1, r2)
    r4 = along_z(2, r2[:64])
    imgs = (pair, r1, r2, r3, r4, q1, q2, sibling(r3), sibling(r4))
    txts = (block, ta, tb, tc)

    vmem = pl.BlockSpec(memory_space=pltpu.VMEM)
    limit = pltpu.CompilerParams(vmem_limit_bytes=16 * 1024 * 1024)
    cost = pl.CostEstimate(flops=2 * 1024 * 1024 * 1152, bytes_accessed=7_000_000, transcendentals=2 * 1024 * 1024)
    w, x, y, sums = pl.pallas_call(
        pair_kernel,
        in_specs=[pl.BlockSpec(memory_space=pltpu.SMEM)] + [vmem] * 13,
        out_specs=[vmem] * 4,
        out_shape=(arr((1024, 1024), BF16), arr((1024, d), BF16), arr((1024, d), BF16), arr((8, 128), F32)),
        compiler_params=limit,
        cost_estimate=cost,
        name="pairs",
    )(scalars, *imgs, *txts)
    sums = sums + sibling(sums)
    w, sums = lax.optimization_barrier((w, sums))

    keep, send = pl.pallas_call(
        image_kernel,
        in_specs=[vmem] * 2,
        out_specs=[vmem] * 2,
        out_shape=(arr((576, d), F32), arr((448, d), F32)),
        compiler_params=limit,
        cost_estimate=cost,
        name="images",
    )(w, y)
    sums = sums + flip_z(1, sums)
    got = sibling(send)
    w, sums, keep = lax.optimization_barrier((w, sums, keep))

    t_own, t_back, t_fore, t_over = pl.pallas_call(
        text_kernel,
        in_specs=[vmem] * 2,
        out_specs=[vmem] * 4,
        out_shape=(arr((256, d), F32),) * 4,
        compiler_params=limit,
        cost_estimate=cost,
        name="texts",
    )(w, x)
    sums = sums + flip_z(2, sums) + flip_z(4, sums) + flip_z(6, sums)

    chain = keep[128:] + got
    g3 = along_z(-1, low(chain[256:384]))
    g4 = along_z(-2, low(chain[384:448]))

    codes = split(sums)
    out = [jnp.concatenate([low(v), codes], axis=0) for v in (t_back, t_fore, t_over)]
    back = [second(k, v).astype(F32) for k, v in zip((-1, 1, 2), out)]
    c2 = chain[128:256] + (g3.astype(F32) + jnp.pad(g4.astype(F32), ((0, 64), (0, 0)))) * UP
    c2, back[0], back[1], back[2] = lax.optimization_barrier((c2, *back))
    t_sum = t_own + (back[0][:256] + back[1][:256] + back[2][:256]) * UP
    sums = sums + sum(join(v[256:]) for v in back)
    codes = split(sums)
    out = [jnp.concatenate([low(t_sum[k * 64 : k * 64 + 64]), codes], axis=0) for k in (1, 2, 3)]
    back = [first(k, v).astype(F32) for k, v in zip((-1, 1, 2), out)]
    txt_dir = t_sum[:64] + (back[0][:64] + back[1][:64] + back[2][:64]) * UP
    sums = sums + sum(join(v[64:]) for v in back)

    g1 = along_z(-1, low(chain[0:128]))
    g2 = along_z(-2, low(c2))
    mine = keep[:128] + (g1.astype(F32) + g2.astype(F32)) * UP
    img_dir = mine[:64] + sibling(mine[64:])

    grad_images, grad_texts = pl.pallas_call(
        project_kernel, out_shape=(arr((rows, d), F32), arr((rows, d), F32)), name="project"
    )(images, texts, img_dir, txt_dir)

    total = float(rows * 256)
    count = total * total
    return (sums[0, 0] / count, grad_images, grad_texts, scale * sums[2, 0] / count, sums[1, 0] / count)


def solution(mesh):
    fine = Mesh(mesh.devices.reshape(SIZES), AXES)
    rows = P(AXES, None)
    return jax.shard_map(
        shards,
        mesh=fine,
        in_specs=(rows, rows, P(), P()),
        out_specs=(P(), rows, rows, P(), P()),
        check_vma=False,
    )
```

```python
import functools
import itertools

import jax
import jax.numpy as jnp
from jax import lax
from jax.experimental import pallas as pl
from jax.experimental.pallas import tpu as pltpu
from jax.sharding import Mesh, PartitionSpec as P

tiny_eps = 1e-06
LOG2E = 1.4426950408889634
LN2 = 0.6931471805599453
F32, BF16, F16 = jnp.float32, jnp.bfloat16, jnp.float16
SHRINK = 2.0**-20
DOWN, UP = 0.125, 8.0

AXES = ("y", "zl", "c", "x", "zh")
SIZES = (4, 4, 2, 4, 2)
COORDS = list(itertools.product(*[range(s) for s in SIZES]))
PLACE = {coord: n for n, coord in enumerate(COORDS)}


def place(y, z, c, x):
    return PLACE[(y % 4, z % 4, c, x % 4, (z % 8) // 4)]


def permute(move, value):
    pairs = []
    for y, zl, c, x, zh in COORDS:
        z = zh * 4 + zl
        pairs.append((place(y, z, c, x), place(*move(y, z, c, x))))
    return lax.ppermute(value, AXES, pairs)


def first(k, v):
    return permute(lambda y, z, c, x: (y, z, c, x + k) if c == 0 else (y + k, z, c, x), v)


def second(k, v):
    return permute(lambda y, z, c, x: (y + k, z, c, x) if c == 0 else (y, z, c, x + k), v)


def along_z(k, v):
    return permute(lambda y, z, c, x: (y, z + k, c, x) if c == 0 else (y, z - k, c, x), v)


def sibling(v):
    return permute(lambda y, z, c, x: (y, z, 1 - c, x), v)


def flip_z(bit, v):
    return permute(lambda y, z, c, x: (y, z ^ bit, c, x), v)


def flip_second(bit, v):
    return permute(lambda y, z, c, x: (y ^ bit, z, c, x) if c == 0 else (y, z, c, x ^ bit), v)


def add_up(messages):
    return sum(m.astype(F32) for m in messages) * UP


def split(sums):
    value = sums * SHRINK
    terms = []
    for _ in range(3):
        term = lax.reduce_precision(value, 5, 10)
        terms.append(term.astype(F16))
        value = (value - term) * 2048.0
    return jnp.pad(jnp.concatenate(terms, axis=1), ((0, 0), (0, 768)))


def join(codes):
    codes = codes.astype(F32)
    return (codes[:, :128] + codes[:, 128:256] / 2048.0 + codes[:, 256:384] / 2048.0**2) / SHRINK


def low(sums):
    return (sums * DOWN).astype(F16)


def unit_rows(wide):
    length = jnp.sqrt(jnp.sum(wide * wide, axis=-1, keepdims=True) + tiny_eps)
    return wide / length, length


def normalise_kernel(images, texts, img_low, txt_low):
    for src, dst in ((images, img_low), (texts, txt_low)):
        unit, _ = unit_rows(src[...].astype(F32))
        dst[...] = unit.astype(BF16)


def fold_rows(value):
    rows, cols = value.shape
    return jnp.sum(value.reshape(rows // 8, 8, cols), axis=0)


def product_rows(value):
    while value.shape[0] > 8:
        half = value.shape[0] // 2
        value = value[:half] * value[half:]
    return value


def lay(pieces, dst):
    at = 0
    for piece in pieces:
        dst[at : at + piece.shape[0], :] = piece[...]
        at += piece.shape[0]


def pair_kernel(sc, *refs):
    imgs, txts = refs[:9], refs[9:13]
    w_ref, x_ref, y_ref, sums = refs[13:]
    lay(imgs, x_ref)
    lay(txts, y_ref)
    scale = sc[0]
    bias = sc[1]
    lift = jnp.zeros((8, 256), F32)
    logs = jnp.zeros((8, 256), F32)
    slope_acc = jnp.zeros((8, 256), F32)
    curve_acc = jnp.zeros((8, 256), F32)
    for j in range(4):
        for i in range(4):
            dots = lax.dot_general(
                x_ref[i * 256 : i * 256 + 256, :],
                y_ref[j * 256 : j * 256 + 256, :],
                (((1,), (1,)), ((), ())),
                preferred_element_type=F32,
            )
            z = (scale * dots + bias) * LOG2E
            if i == 0 and j == 0:
                row = lax.broadcasted_iota(jnp.int32, (256, 256), 0)
                col = lax.broadcasted_iota(jnp.int32, (256, 256), 1)
                positive = jnp.logical_and(row == col, row < 64)
                z = jnp.where(positive, -z, z)
            e = jnp.exp2(-jnp.abs(z))
            whole = 1.0 + e
            r = 1.0 / whole
            slope = jnp.where(z >= 0.0, r, e * r)
            if i == 0 and j == 0:
                slope = jnp.where(positive, -slope, slope)
            lift += fold_rows(jnp.maximum(z, 0.0))
            logs += jnp.log(product_rows(whole))
            slope_acc += fold_rows(slope)
            curve_acc += fold_rows(slope * dots)
            w_ref[i * 256 : i * 256 + 256, j * 256 : j * 256 + 256] = (scale * slope).astype(BF16)
    loss = LN2 * jnp.sum(lift) + jnp.sum(logs)
    row = lax.broadcasted_iota(jnp.int32, (8, 128), 0)
    sums[...] = jnp.where(
        row == 0, loss, jnp.where(row == 1, jnp.sum(slope_acc), jnp.where(row == 2, jnp.sum(curve_acc), 0.0))
    )


def image_kernel(w_ref, y_ref, keep, send):
    for lo, hi in ((576, 800), (800, 1024)):
        send[lo - 576 : hi - 576, :] = jnp.dot(w_ref[lo:hi, :], y_ref[...], preferred_element_type=F32)
    for lo, hi in ((0, 288), (288, 576)):
        keep[lo:hi, :] = jnp.dot(w_ref[lo:hi, :], y_ref[...], preferred_element_type=F32)


def text_kernel(w_ref, x_ref, own, back, fore, over):
    for j, out in ((1, back), (2, fore), (3, over), (0, own)):
        out[...] = lax.dot_general(
            w_ref[:, j * 256 : j * 256 + 256], x_ref[...], (((0,), (0,)), ((), ())), preferred_element_type=F32
        )


def project_kernel(values, sums, grads):
    unit, length = unit_rows(values[...].astype(F32))
    direction = sums[...]
    along = jnp.sum(unit * direction, axis=-1, keepdims=True)
    grads[...] = (direction - unit * along) / length


def finish_kernel(share, sc, images, img_dir, sums, grads, mean_loss, grad_log_scale, grad_bias):
    project_kernel(images, img_dir, grads)
    mean_loss[0] = sums[0, 0] * share
    grad_bias[0] = sums[1, 0] * share
    grad_log_scale[0] = sc[0] * (sums[2, 0] * share)


def shards(images, texts, log_scale, bias):
    rows, d = images.shape
    arr = jax.ShapeDtypeStruct
    small = pltpu.CompilerParams(vmem_limit_bytes=4 * 1024 * 1024)
    img_low, txt_low = pl.pallas_call(
        normalise_kernel,
        out_shape=(arr((rows, d), BF16), arr((rows, d), BF16)),
        compiler_params=small,
        name="normalise",
    )(images, texts)
    pair = jnp.concatenate([img_low, sibling(img_low)], axis=0)
    scale = jnp.exp(log_scale)
    scalars = jnp.stack([scale, bias])

    pair, txt_low = lax.optimization_barrier((pair, txt_low))
    r2 = along_z(2, pair)
    a, b, c = first(1, txt_low), first(-1, txt_low), first(2, txt_low)
    block = jnp.concatenate([txt_low, a, b, c], axis=0)
    block, pair = lax.optimization_barrier((block, pair))
    ta, tb, tc = second(1, block), second(-1, block), second(2, block)
    r1 = along_z(1, pair)
    q1, q2 = sibling(r1), sibling(r2)
    r2, q2 = lax.optimization_barrier((r2, q2))
    r3 = along_z(1, r2)
    r4 = along_z(2, r2[:64])
    imgs = (pair, r1, r3, r2, r4, q1, sibling(r3), q2, sibling(r4))
    txts = (block, ta, tb, tc)

    vmem = pl.BlockSpec(memory_space=pltpu.VMEM)
    limit = pltpu.CompilerParams(vmem_limit_bytes=16 * 1024 * 1024)
    cost = pl.CostEstimate(flops=2 * 1024 * 1024 * 1152, bytes_accessed=7_000_000, transcendentals=2 * 1024 * 1024)
    w, x, y, sums = pl.pallas_call(
        pair_kernel,
        in_specs=[pl.BlockSpec(memory_space=pltpu.SMEM)] + [vmem] * 13,
        out_specs=[vmem] * 4,
        out_shape=(arr((1024, 1024), BF16), arr((1024, d), BF16), arr((1024, d), BF16), arr((8, 128), F32)),
        compiler_params=limit,
        cost_estimate=cost,
        name="pairs",
    )(scalars, *imgs, *txts)

    sums = sums + sibling(sums)
    w, sums = lax.optimization_barrier((w, sums))
    keep, send = pl.pallas_call(
        image_kernel,
        in_specs=[vmem] * 2,
        out_specs=[vmem] * 2,
        out_shape=(arr((576, d), F32), arr((448, d), F32)),
        compiler_params=limit,
        cost_estimate=cost,
        name="images",
    )(w, y)
    sums = sums + flip_z(4, sums)
    w, keep = lax.optimization_barrier((w, keep))
    t_own, t_back, t_fore, t_over = pl.pallas_call(
        text_kernel,
        in_specs=[vmem] * 2,
        out_specs=[vmem] * 4,
        out_shape=(arr((256, d), F32),) * 4,
        compiler_params=limit,
        cost_estimate=cost,
        name="texts",
    )(w, x)

    codes = split(sums)
    out = [jnp.concatenate([low(v), codes], axis=0) for v in (t_back, t_fore, t_over)]
    back = [second(k, v) for k, v in zip((-1, 1, 2), out)]

    chain = keep[128:] + sibling(send)
    z1 = along_z(-1, low(chain[:256]))
    z4 = along_z(-2, low(chain[384:]))

    c2 = low(chain[256:384] + (z1[128:].astype(F32) + jnp.pad(z4.astype(F32), ((0, 64), (0, 0)))) * UP)
    *back, _, _ = lax.optimization_barrier((*back, z1, z4))
    z2 = along_z(-2, c2)
    t_sum = t_own + add_up(v[:256] for v in back)
    sums = sums + sum(join(v[256:]) for v in back)
    codes = split(sums)
    out = [jnp.concatenate([low(t_sum[k * 64 : k * 64 + 64]), codes], axis=0) for k in (1, 2, 3)]
    back = [first(k, v) for k, v in zip((-1, 1, 2), out)]

    mine = keep[:128] + add_up((z1[:128], z2))
    img_dir = mine[:64] + sibling(mine[64:])

    txt_dir = t_sum[:64] + add_up(v[:64] for v in back)
    sums = sums + sum(join(v[64:]) for v in back)
    sums = sums + flip_z(1, sums) + flip_z(2, sums) + flip_z(3, sums)

    project = pl.pallas_call(project_kernel, out_shape=arr((rows, d), F32), compiler_params=small, name="project")
    grad_texts = project(texts, txt_dir)
    total = float(rows * 256)
    one = pl.BlockSpec(memory_space=pltpu.SMEM)
    grad_images, *means = pl.pallas_call(
        functools.partial(finish_kernel, 1.0 / (total * total)),
        in_specs=[one] + [vmem] * 3,
        out_specs=[vmem] + [one] * 3,
        out_shape=[arr((rows, d), F32)] + [arr((1,), F32)] * 3,
        compiler_params=small,
        name="finish",
    )(scalars, images, img_dir, sums)
    mean_loss, grad_log_scale, grad_bias = (m.reshape(()) for m in means)
    return (mean_loss, grad_images, grad_texts, grad_log_scale, grad_bias)


def solution(mesh):
    fine = Mesh(mesh.devices.reshape(SIZES), AXES)
    rows = P(AXES, None)
    return jax.shard_map(
        shards,
        mesh=fine,
        in_specs=(rows, rows, P(), P()),
        out_specs=(P(), rows, rows, P(), P()),
        check_vma=False,
    )
```

```python
import functools
import itertools

import jax
import jax.numpy as jnp
from jax import lax
from jax.experimental import pallas as pl
from jax.experimental.pallas import tpu as pltpu
from jax.sharding import Mesh, PartitionSpec as P

tiny_eps = 1e-06
LOG2E = 1.4426950408889634
LN2 = 0.6931471805599453
F32, BF16, F16 = jnp.float32, jnp.bfloat16, jnp.float16
SHRINK = 2.0**-20
DOWN, UP = 0.125, 8.0

AXES = ("y", "zl", "c", "x", "zh")
SIZES = (4, 4, 2, 4, 2)
COORDS = list(itertools.product(*[range(s) for s in SIZES]))
PLACE = {coord: n for n, coord in enumerate(COORDS)}


def place(y, z, c, x):
    return PLACE[(y % 4, z % 4, c, x % 4, (z % 8) // 4)]


def permute(move, value):
    pairs = []
    for y, zl, c, x, zh in COORDS:
        z = zh * 4 + zl
        pairs.append((place(y, z, c, x), place(*move(y, z, c, x))))
    return lax.ppermute(value, AXES, pairs)


def first(k, v):
    return permute(lambda y, z, c, x: (y, z, c, x + k) if c == 0 else (y + k, z, c, x), v)


def second(k, v):
    return permute(lambda y, z, c, x: (y + k, z, c, x) if c == 0 else (y, z, c, x + k), v)


def along_z(k, v):
    return permute(lambda y, z, c, x: (y, z + k, c, x) if c == 0 else (y, z - k, c, x), v)


def sibling(v):
    return permute(lambda y, z, c, x: (y, z, 1 - c, x), v)


def flip_z(bit, v):
    return permute(lambda y, z, c, x: (y, z ^ bit, c, x), v)


def flip_second(bit, v):
    return permute(lambda y, z, c, x: (y ^ bit, z, c, x) if c == 0 else (y, z, c, x ^ bit), v)


def add_up(messages):
    return sum(m.astype(F32) for m in messages) * UP


def split(sums):
    value = sums * SHRINK
    terms = []
    for _ in range(3):
        term = lax.reduce_precision(value, 5, 10)
        terms.append(term.astype(F16))
        value = (value - term) * 2048.0
    return jnp.pad(jnp.concatenate(terms, axis=1), ((0, 0), (0, 768)))


def join(codes):
    codes = codes.astype(F32)
    return (codes[:, :128] + codes[:, 128:256] / 2048.0 + codes[:, 256:384] / 2048.0**2) / SHRINK


def low(sums):
    return (sums * DOWN).astype(F16)


def unit_rows(wide):
    length = jnp.sqrt(jnp.sum(wide * wide, axis=-1, keepdims=True) + tiny_eps)
    return wide / length, length


def normalise_kernel(images, texts, img_low, txt_low):
    for src, dst in ((images, img_low), (texts, txt_low)):
        unit, _ = unit_rows(src[...].astype(F32))
        dst[...] = unit.astype(BF16)


def fold_rows(value):
    rows, cols = value.shape
    return jnp.sum(value.reshape(rows // 8, 8, cols), axis=0)


def product_rows(value):
    while value.shape[0] > 8:
        half = value.shape[0] // 2
        value = value[:half] * value[half:]
    return value


def lay(pieces, dst):
    at = 0
    for piece in pieces:
        dst[at : at + piece.shape[0], :] = piece[...]
        at += piece.shape[0]


def pair_kernel(sc, *refs):
    imgs, txts = refs[:9], refs[9:13]
    w_ref, x_ref, y_ref, sums = refs[13:]
    lay(imgs, x_ref)
    lay(txts, y_ref)
    scale = sc[0]
    slant = scale * LOG2E
    offset = sc[1] * LOG2E
    lift = jnp.zeros((8, 256), F32)
    logs = jnp.zeros((8, 256), F32)
    slope_acc = jnp.zeros((8, 256), F32)
    curve_acc = jnp.zeros((8, 256), F32)
    for j in range(4):
        for i in range(4):
            dots = lax.dot_general(
                x_ref[i * 256 : i * 256 + 256, :],
                y_ref[j * 256 : j * 256 + 256, :],
                (((1,), (1,)), ((), ())),
                preferred_element_type=F32,
            )
            z = slant * dots + offset
            if i == 0 and j == 0:
                row = lax.broadcasted_iota(jnp.int32, (256, 256), 0)
                col = lax.broadcasted_iota(jnp.int32, (256, 256), 1)
                positive = jnp.logical_and(row == col, row < 64)
                z = jnp.where(positive, -z, z)
            e = jnp.exp2(-jnp.abs(z))
            whole = 1.0 + e
            r = 1.0 / whole
            slope = jnp.where(z >= 0.0, r, e * r)
            if i == 0 and j == 0:
                slope = jnp.where(positive, -slope, slope)
            lift += fold_rows(jnp.maximum(z, 0.0))
            logs += jnp.log(product_rows(whole))
            slope_acc += fold_rows(slope)
            curve_acc += fold_rows(slope * dots)
            w_ref[i * 256 : i * 256 + 256, j * 256 : j * 256 + 256] = (scale * slope).astype(BF16)
    loss = LN2 * jnp.sum(lift) + jnp.sum(logs)
    row = lax.broadcasted_iota(jnp.int32, (8, 128), 0)
    sums[...] = jnp.where(
        row == 0, loss, jnp.where(row == 1, jnp.sum(slope_acc), jnp.where(row == 2, jnp.sum(curve_acc), 0.0))
    )


def image_kernel(w_ref, y_ref, keep, send):
    for lo, hi in ((576, 800), (800, 1024)):
        send[lo - 576 : hi - 576, :] = jnp.dot(w_ref[lo:hi, :], y_ref[...], preferred_element_type=F32)
    for lo, hi in ((0, 288), (288, 576)):
        keep[lo:hi, :] = jnp.dot(w_ref[lo:hi, :], y_ref[...], preferred_element_type=F32)


def text_kernel(w_ref, x_ref, own, back, fore, over):
    for j, out in ((1, back), (2, fore), (3, over), (0, own)):
        out[...] = lax.dot_general(
            w_ref[:, j * 256 : j * 256 + 256], x_ref[...], (((0,), (0,)), ((), ())), preferred_element_type=F32
        )


def project_kernel(values, sums, grads):
    unit, length = unit_rows(values[...].astype(F32))
    direction = sums[...]
    along = jnp.sum(unit * direction, axis=-1, keepdims=True)
    grads[...] = (direction - unit * along) / length


def finish_kernel(share, sc, images, img_dir, sums, grads, mean_loss, grad_log_scale, grad_bias):
    project_kernel(images, img_dir, grads)
    mean_loss[0] = sums[0, 0] * share
    grad_bias[0] = sums[1, 0] * share
    grad_log_scale[0] = sc[0] * (sums[2, 0] * share)


def shards(images, texts, log_scale, bias):
    rows, d = images.shape
    arr = jax.ShapeDtypeStruct
    small = pltpu.CompilerParams(vmem_limit_bytes=4 * 1024 * 1024)
    img_low, txt_low = pl.pallas_call(
        normalise_kernel,
        out_shape=(arr((rows, d), BF16), arr((rows, d), BF16)),
        compiler_params=small,
        name="normalise",
    )(images, texts)
    pair = jnp.concatenate([img_low, sibling(img_low)], axis=0)
    scale = jnp.exp(log_scale)
    scalars = jnp.stack([scale, bias])

    pair, txt_low = lax.optimization_barrier((pair, txt_low))
    r2 = along_z(2, pair)
    a, b, c = first(1, txt_low), first(-1, txt_low), first(2, txt_low)
    block = jnp.concatenate([txt_low, a, b, c], axis=0)
    block, pair = lax.optimization_barrier((block, pair))
    ta, tb, tc = second(1, block), second(-1, block), second(2, block)
    r1 = along_z(1, pair)
    q1, q2 = sibling(r1), sibling(r2)
    r2, q2 = lax.optimization_barrier((r2, q2))
    r3 = along_z(1, r2)
    r4 = along_z(2, r2[:64])
    imgs = (pair, r1, r3, r2, r4, q1, sibling(r3), q2, sibling(r4))
    txts = (block, ta, tb, tc)

    vmem = pl.BlockSpec(memory_space=pltpu.VMEM)
    limit = pltpu.CompilerParams(vmem_limit_bytes=16 * 1024 * 1024)
    cost = pl.CostEstimate(flops=2 * 1024 * 1024 * 1152, bytes_accessed=7_000_000, transcendentals=2 * 1024 * 1024)
    w, x, y, sums = pl.pallas_call(
        pair_kernel,
        in_specs=[pl.BlockSpec(memory_space=pltpu.SMEM)] + [vmem] * 13,
        out_specs=[vmem] * 4,
        out_shape=(arr((1024, 1024), BF16), arr((1024, d), BF16), arr((1024, d), BF16), arr((8, 128), F32)),
        compiler_params=limit,
        cost_estimate=cost,
        name="pairs",
    )(scalars, *imgs, *txts)

    sums = sums + flip_z(4, sums)
    keep, send = pl.pallas_call(
        image_kernel,
        in_specs=[vmem] * 2,
        out_specs=[vmem] * 2,
        out_shape=(arr((576, d), F32), arr((448, d), F32)),
        compiler_params=limit,
        cost_estimate=cost,
        name="images",
    )(w, y)
    w, keep, sums = lax.optimization_barrier((w, keep, sums))
    sums = sums + sibling(sums)
    t_own, t_back, t_fore, t_over = pl.pallas_call(
        text_kernel,
        in_specs=[vmem] * 2,
        out_specs=[vmem] * 4,
        out_shape=(arr((256, d), F32),) * 4,
        compiler_params=limit,
        cost_estimate=cost,
        name="texts",
    )(w, x)

    codes = split(sums)
    out = [jnp.concatenate([low(v), codes], axis=0) for v in (t_back, t_fore, t_over)]
    back = [second(k, v) for k, v in zip((-1, 1, 2), out)]

    chain = keep[128:] + sibling(send)
    z1 = along_z(-1, low(chain[:256]))
    z4 = along_z(-2, low(chain[384:]))

    c2 = low(chain[256:384] + (z1[128:].astype(F32) + jnp.pad(z4.astype(F32), ((0, 64), (0, 0)))) * UP)
    *back, _, _ = lax.optimization_barrier((*back, z1, z4))
    z2 = along_z(-2, c2)
    t_sum = t_own + add_up(v[:256] for v in back)
    sums = sums + sum(join(v[256:]) for v in back)
    codes = split(sums)
    out = [jnp.concatenate([low(t_sum[k * 64 : k * 64 + 64]), codes], axis=0) for k in (1, 2, 3)]
    back = [first(k, v) for k, v in zip((-1, 1, 2), out)]

    mine = keep[:128] + add_up((z1[:128], z2))
    img_dir = mine[:64] + sibling(mine[64:])

    txt_dir = t_sum[:64] + add_up(v[:64] for v in back)
    sums = sums + sum(join(v[64:]) for v in back)
    sums = sums + flip_z(1, sums) + flip_z(2, sums) + flip_z(3, sums)

    project = pl.pallas_call(project_kernel, out_shape=arr((rows, d), F32), compiler_params=small, name="project")
    grad_texts = project(texts, txt_dir)
    total = float(rows * 256)
    one = pl.BlockSpec(memory_space=pltpu.SMEM)
    grad_images, *means = pl.pallas_call(
        functools.partial(finish_kernel, 1.0 / (total * total)),
        in_specs=[one] + [vmem] * 3,
        out_specs=[vmem] + [one] * 3,
        out_shape=[arr((rows, d), F32)] + [arr((1,), F32)] * 3,
        compiler_params=small,
        name="finish",
    )(scalars, images, img_dir, sums)
    mean_loss, grad_log_scale, grad_bias = (m.reshape(()) for m in means)
    return (mean_loss, grad_images, grad_texts, grad_log_scale, grad_bias)


def solution(mesh):
    fine = Mesh(mesh.devices.reshape(SIZES), AXES)
    rows = P(AXES, None)
    return jax.shard_map(
        shards,
        mesh=fine,
        in_specs=(rows, rows, P(), P()),
        out_specs=(P(), rows, rows, P(), P()),
        check_vma=False,
    )
```

```python
import functools
import itertools

import jax
import jax.numpy as jnp
from jax import lax
from jax.experimental import pallas as pl
from jax.experimental.pallas import tpu as pltpu
from jax.sharding import Mesh, PartitionSpec as P

tiny_eps = 1e-06
LOG2E = 1.4426950408889634
LN2 = 0.6931471805599453
F32, BF16, F16 = jnp.float32, jnp.bfloat16, jnp.float16
SHRINK = 2.0**-20
DOWN, UP = 0.125, 8.0

AXES = ("y", "zl", "c", "x", "zh")
SIZES = (4, 4, 2, 4, 2)
COORDS = list(itertools.product(*[range(s) for s in SIZES]))
PLACE = {coord: n for n, coord in enumerate(COORDS)}


def place(y, z, c, x):
    return PLACE[(y % 4, z % 4, c, x % 4, (z % 8) // 4)]


def permute(move, value):
    pairs = []
    for y, zl, c, x, zh in COORDS:
        z = zh * 4 + zl
        pairs.append((place(y, z, c, x), place(*move(y, z, c, x))))
    return lax.ppermute(value, AXES, pairs)


def first(k, v):
    return permute(lambda y, z, c, x: (y, z, c, x + k) if c == 0 else (y + k, z, c, x), v)


def second(k, v):
    return permute(lambda y, z, c, x: (y + k, z, c, x) if c == 0 else (y, z, c, x + k), v)


def along_z(k, v):
    return permute(lambda y, z, c, x: (y, z + k, c, x) if c == 0 else (y, z - k, c, x), v)


def sibling(v):
    return permute(lambda y, z, c, x: (y, z, 1 - c, x), v)


def flip_z(bit, v):
    return permute(lambda y, z, c, x: (y, z ^ bit, c, x), v)


def flip_second(bit, v):
    return permute(lambda y, z, c, x: (y ^ bit, z, c, x) if c == 0 else (y, z, c, x ^ bit), v)


def add_up(messages):
    return sum(m.astype(F32) for m in messages) * UP


def split(sums):
    value = sums * SHRINK
    terms = []
    for _ in range(3):
        term = lax.reduce_precision(value, 5, 10)
        terms.append(term.astype(F16))
        value = (value - term) * 2048.0
    return jnp.pad(jnp.concatenate(terms, axis=1), ((0, 0), (0, 768)))


def join(codes):
    codes = codes.astype(F32)
    return (codes[:, :128] + codes[:, 128:256] / 2048.0 + codes[:, 256:384] / 2048.0**2) / SHRINK


def low(sums):
    return (sums * DOWN).astype(F16)


def unit_rows(wide):
    length = jnp.sqrt(jnp.sum(wide * wide, axis=-1, keepdims=True) + tiny_eps)
    return wide / length, length


def normalise_kernel(images, texts, img_low, txt_low):
    for src, dst in ((images, img_low), (texts, txt_low)):
        unit, _ = unit_rows(src[...].astype(F32))
        dst[...] = unit.astype(BF16)


def fold_rows(value):
    rows, cols = value.shape
    return jnp.sum(value.reshape(rows // 8, 8, cols), axis=0)


def product_rows(value):
    while value.shape[0] > 8:
        half = value.shape[0] // 2
        value = value[:half] * value[half:]
    return value


def lay(pieces, dst):
    at = 0
    for piece in pieces:
        dst[at : at + piece.shape[0], :] = piece[...]
        at += piece.shape[0]


def pair_kernel(sc, *refs):
    imgs, txts = refs[:9], refs[9:13]
    w_ref, x_ref, y_ref, sums = refs[13:]
    lay(imgs, x_ref)
    lay(txts, y_ref)
    scale = sc[0]
    slant = scale * LOG2E
    offset = sc[1] * LOG2E
    lift = jnp.zeros((8, 256), F32)
    logs = jnp.zeros((8, 256), F32)
    slope_acc = jnp.zeros((8, 256), F32)
    curve_acc = jnp.zeros((8, 256), F32)
    for j in range(4):
        for i in range(4):
            dots = lax.dot_general(
                x_ref[i * 256 : i * 256 + 256, :],
                y_ref[j * 256 : j * 256 + 256, :],
                (((1,), (1,)), ((), ())),
                preferred_element_type=F32,
            )
            z = slant * dots + offset
            if i == 0 and j == 0:
                row = lax.broadcasted_iota(jnp.int32, (256, 256), 0)
                col = lax.broadcasted_iota(jnp.int32, (256, 256), 1)
                positive = jnp.logical_and(row == col, row < 64)
                z = jnp.where(positive, -z, z)
            e = jnp.exp2(-jnp.abs(z))
            whole = 1.0 + e
            r = 1.0 / whole
            slope = jnp.where(z >= 0.0, r, e * r)
            if i == 0 and j == 0:
                slope = jnp.where(positive, -slope, slope)
            lift += fold_rows(jnp.maximum(z, 0.0))
            logs += jnp.log(product_rows(whole))
            slope_acc += fold_rows(slope)
            curve_acc += fold_rows(slope * dots)
            w_ref[i * 256 : i * 256 + 256, j * 256 : j * 256 + 256] = (scale * slope).astype(BF16)
    loss = LN2 * jnp.sum(lift) + jnp.sum(logs)
    row = lax.broadcasted_iota(jnp.int32, (8, 128), 0)
    sums[...] = jnp.where(
        row == 0, loss, jnp.where(row == 1, jnp.sum(slope_acc), jnp.where(row == 2, jnp.sum(curve_acc), 0.0))
    )


def image_kernel(w_ref, y_ref, keep, send):
    for lo, hi in ((576, 800), (800, 1024)):
        send[lo - 576 : hi - 576, :] = jnp.dot(w_ref[lo:hi, :], y_ref[...], preferred_element_type=F32)
    for lo, hi in ((0, 288), (288, 576)):
        keep[lo:hi, :] = jnp.dot(w_ref[lo:hi, :], y_ref[...], preferred_element_type=F32)


def text_kernel(w_ref, x_ref, own, back, fore, over):
    for j, out in ((1, back), (2, fore), (3, over), (0, own)):
        out[...] = lax.dot_general(
            w_ref[:, j * 256 : j * 256 + 256], x_ref[...], (((0,), (0,)), ((), ())), preferred_element_type=F32
        )


def project_kernel(values, sums, grads):
    unit, length = unit_rows(values[...].astype(F32))
    direction = sums[...]
    along = jnp.sum(unit * direction, axis=-1, keepdims=True)
    grads[...] = (direction - unit * along) / length


def finish_kernel(share, sc, images, img_dir, sums, grads, mean_loss, grad_log_scale, grad_bias):
    project_kernel(images, img_dir, grads)
    mean_loss[0] = sums[0, 0] * share
    grad_bias[0] = sums[1, 0] * share
    grad_log_scale[0] = sc[0] * (sums[2, 0] * share)


def shards(images, texts, log_scale, bias):
    rows, d = images.shape
    arr = jax.ShapeDtypeStruct
    small = pltpu.CompilerParams(vmem_limit_bytes=4 * 1024 * 1024)
    img_low, txt_low = pl.pallas_call(
        normalise_kernel,
        out_shape=(arr((rows, d), BF16), arr((rows, d), BF16)),
        compiler_params=small,
        name="normalise",
    )(images, texts)
    pair = jnp.concatenate([img_low, sibling(img_low)], axis=0)
    scale = jnp.exp(log_scale)
    scalars = jnp.stack([scale, bias])

    pair, txt_low = lax.optimization_barrier((pair, txt_low))
    r2 = along_z(2, pair)
    a, b, c = first(1, txt_low), first(-1, txt_low), first(2, txt_low)
    block = jnp.concatenate([txt_low, a, b, c], axis=0)
    block, pair = lax.optimization_barrier((block, pair))
    tc = second(2, block)
    ta, tb = second(1, block), second(-1, block)
    r1 = along_z(1, pair)
    q1, q2 = sibling(r1), sibling(r2)
    r2, q2 = lax.optimization_barrier((r2, q2))
    r3 = along_z(1, r2)
    r4 = along_z(2, r2[:64])
    imgs = (pair, r1, r3, r2, r4, q1, sibling(r3), q2, sibling(r4))
    txts = (block, ta, tb, tc)

    vmem = pl.BlockSpec(memory_space=pltpu.VMEM)
    limit = pltpu.CompilerParams(vmem_limit_bytes=16 * 1024 * 1024)
    cost = pl.CostEstimate(flops=2 * 1024 * 1024 * 1152, bytes_accessed=7_000_000, transcendentals=2 * 1024 * 1024)
    w, x, y, sums = pl.pallas_call(
        pair_kernel,
        in_specs=[pl.BlockSpec(memory_space=pltpu.SMEM)] + [vmem] * 13,
        out_specs=[vmem] * 4,
        out_shape=(arr((1024, 1024), BF16), arr((1024, d), BF16), arr((1024, d), BF16), arr((8, 128), F32)),
        compiler_params=limit,
        cost_estimate=cost,
        name="pairs",
    )(scalars, *imgs, *txts)

    sums = sums + flip_z(4, sums)
    keep, send = pl.pallas_call(
        image_kernel,
        in_specs=[vmem] * 2,
        out_specs=[vmem] * 2,
        out_shape=(arr((576, d), F32), arr((448, d), F32)),
        compiler_params=limit,
        cost_estimate=cost,
        name="images",
    )(w, y)
    w, keep, sums = lax.optimization_barrier((w, keep, sums))
    sums = sums + sibling(sums)
    t_own, t_back, t_fore, t_over = pl.pallas_call(
        text_kernel,
        in_specs=[vmem] * 2,
        out_specs=[vmem] * 4,
        out_shape=(arr((256, d), F32),) * 4,
        compiler_params=limit,
        cost_estimate=cost,
        name="texts",
    )(w, x)

    codes = split(sums)
    out = [jnp.concatenate([low(v), codes], axis=0) for v in (t_back, t_fore, t_over)]
    back = [second(k, v) for k, v in zip((2, -1, 1), (out[2], out[0], out[1]))]

    chain = keep[128:] + sibling(low(send)).astype(F32) * UP
    z1 = along_z(-1, low(chain[:256]))
    z4 = along_z(-2, low(chain[384:]))

    c2 = low(chain[256:384] + (z1[128:].astype(F32) + jnp.pad(z4.astype(F32), ((0, 64), (0, 0)))) * UP)
    *back, _, _ = lax.optimization_barrier((*back, z1, z4))
    z2 = along_z(-2, c2)
    t_sum = t_own + add_up(v[:256] for v in back)
    sums = sums + sum(join(v[256:]) for v in back)
    codes = split(sums)
    out = [jnp.concatenate([low(t_sum[k * 64 : k * 64 + 64]), codes], axis=0) for k in (1, 2, 3)]
    back = [first(k, v) for k, v in zip((-1, 1, 2), out)]

    mine = keep[:128] + add_up((z1[:128], z2))
    img_dir = mine[:64] + sibling(mine[64:])

    txt_dir = t_sum[:64] + add_up(v[:64] for v in back)
    sums = sums + sum(join(v[64:]) for v in back)
    sums = sums + flip_z(1, sums) + flip_z(2, sums) + flip_z(3, sums)

    project = pl.pallas_call(project_kernel, out_shape=arr((rows, d), F32), compiler_params=small, name="project")
    grad_texts = project(texts, txt_dir)
    total = float(rows * 256)
    one = pl.BlockSpec(memory_space=pltpu.SMEM)
    grad_images, *means = pl.pallas_call(
        functools.partial(finish_kernel, 1.0 / (total * total)),
        in_specs=[one] + [vmem] * 3,
        out_specs=[vmem] + [one] * 3,
        out_shape=[arr((rows, d), F32)] + [arr((1,), F32)] * 3,
        compiler_params=small,
        name="finish",
    )(scalars, images, img_dir, sums)
    mean_loss, grad_log_scale, grad_bias = (m.reshape(()) for m in means)
    return (mean_loss, grad_images, grad_texts, grad_log_scale, grad_bias)


def solution(mesh):
    fine = Mesh(mesh.devices.reshape(SIZES), AXES)
    rows = P(AXES, None)
    return jax.shard_map(
        shards,
        mesh=fine,
        in_specs=(rows, rows, P(), P()),
        out_specs=(P(), rows, rows, P(), P()),
        check_vma=False,
    )
```
